32 devices in a mesh: groups: 1, expert: 8 (over z, y), tensor: 2 (over x), pair: 2 (over core).
Axes of the slice: x: 2, y: 2, z: 4, core: 2. Of those that a mesh axis runs over, the one named last changes fastest.
Arguments:
- tokens: bfloat16 [512, 3584], P(('groups', 'expert', 'tensor', 'pair')), may hold values from -6 to 6
- expert_ids: int32 [512, 8], P(('groups', 'expert', 'tensor', 'pair')), may hold values from 0 to 15, all different within a row; in each aligned block of 16 rows (0 to 15, 16 to 31, ...) at most 16 rows name the same one
- route_weight: float32 [512, 8], P(('groups', 'expert', 'tensor', 'pair')), may hold values from 0.05 to 0.5
- w_gate: bfloat16 [16, 3584, 1024], P(('expert', 'pair'), None, 'tensor'), may hold values from -0.09375 to 0.09375
- w_up: bfloat16 [16, 3584, 1024], P(('expert', 'pair'), None, 'tensor'), may hold values from -0.09375 to 0.09375
- w_down: bfloat16 [16, 1024, 3584], P(('expert', 'pair'), 'tensor'), may hold values from -0.1875 to 0.1875
- s_gate: bfloat16 [3584, 2048], P(None, ('tensor', 'pair')), may hold values from -0.09375 to 0.09375
- s_up: bfloat16 [3584, 2048], P(None, ('tensor', 'pair')), may hold values from -0.09375 to 0.09375
- s_down: bfloat16 [2048, 3584], P(('tensor', 'pair')), may hold values from -0.125 to 0.125
Outputs:
- moe_out: bfloat16 [512, 3584], P(('groups', 'expert', 'tensor', 'pair'))
The draws below stay inside these ranges and needn't reach their ends.
Inputs may be any that keep to these rules, and one draw needn't show every extreme that they name: `expert_ids`: each row names 8 different experts. Among the 16 tokens of one device no expert is named by more than 16 tokens, and in every draw some expert is named by exactly 16 tokens of some device.
All inputs are finite; a program needn't handle non-finite values.
Results may differ from the reference program's by a relative error of at most 0.014.
Values may be sent and summed in bfloat16 or wider, within the bound.
No kernel may reach another device: no remote copies, remote signals or barrier semaphores. Data moves between devices by JAX's collectives and lax.ppermute only.
A program may use at most 64 MiB of HBM per device.

```python
import math
import jax
import jax.numpy as jnp
import numpy as np
from jax import lax

D = 3584
EH = 1024
SH = 2048
TOP = 8
TOK_DEV = 16
EXPERTS = 16
CAP = 16
TOKENS = 512
N_EXPERT = 8
N_TENSOR = 2
N_PAIR = 2


def block_levels(key, dims, cuts, smallest, largest):
    level, own = 1.0, jax.random.fold_in(key, 6)
    for dim, parts in cuts:
        steps = jnp.exp(jax.random.uniform(jax.random.fold_in(own, dim), (parts,), jnp.float32, smallest / len(cuts), largest / len(cuts)))
        level = level * jnp.repeat(steps, dims[dim] // parts).reshape([-1 if axis == dim else 1 for axis in range(len(dims))])
    return level


def routed_block(rng, own, number, rows, amount, top, bound, slope):
    ranking = jax.random.permutation(rng, amount)
    heavy_load, ordinary = portions_of(amount, rows * top, bound, slope, True), portions_of(amount, rows * top, bound, slope, False)
    places = jnp.arange(amount)

    def named(lengths, turn):
        used = int((lengths > 0).sum())
        fixed = max(1, used // 4)
        passed = fixed + (places - fixed + turn * (used - fixed)) % max(1, amount - fixed)
        return jnp.zeros((amount,), jnp.int32).at[ranking[jnp.where(places < fixed, places, passed)]].set(jnp.asarray(lengths, jnp.int32))

    lengths = jnp.where(number % 4 == 0, named(heavy_load, number // 4), named(ordinary, number - number // 4 - 1))
    mixed = jax.random.permutation(jax.random.fold_in(own, 3), amount)
    donor, sink = mixed[0:amount // 2 * 2:2], mixed[1:amount // 2 * 2:2]
    room = jnp.minimum(lengths[donor] - 1, bound - lengths[sink]) // 2
    room = jnp.where((donor == ranking[0]) | (sink == ranking[0]) | (lengths[sink] == 0), 0, jnp.maximum(room, 0))
    passed = jax.random.randint(jax.random.fold_in(own, 4), (amount // 2,), 0, 1 << 20) % (room + 1)
    lengths = lengths.at[donor].add(-passed).at[sink].add(passed)
    items = jnp.searchsorted(jnp.cumsum(lengths), jnp.arange(rows * top), side="right").astype(jnp.int32)
    grid = items.reshape(top, rows).T
    grid = grid[jax.random.permutation(jax.random.fold_in(own, 1), rows)]
    turn = jax.random.randint(jax.random.fold_in(own, 2), (rows, 1), 0, top)
    return jnp.take_along_axis(grid, (jnp.arange(top)[None, :] + turn) % top, axis=1)


def portions_of(count, total, limit, lean, full):
    weights = [(1 << 20) // math.isqrt(standing ** lean) + 1 for standing in range(1, count + 1)]
    largest = limit if full else min(limit, max(-(-total // count), total * weights[0] // sum(weights)))
    least = 1 if total - largest >= count - 1 else 0
    holding, surplus = [largest] + [least] * (count - 1), total - largest - least * (count - 1)
    while surplus > 0:
        candidates = [i for i in range(1, count) if holding[i] < largest] or [i for i in range(1, count) if holding[i] < limit]
        mass, left = sum([weights[i] for i in candidates]), surplus
        for i in candidates:
            addition = min(limit - holding[i], max(1, left * weights[i] // mass), surplus)
            holding[i] = holding[i] + addition
            surplus = surplus - addition
    return np.array(holding)


def centred(own_key, shape, scale, limit, cuts=(), kind=jnp.bfloat16):
    values = scale * jax.random.normal(own_key, shape, jnp.float32)
    if cuts:
        values = values * block_levels(own_key, shape, cuts, -0.22, 0.18)
    return jnp.clip(values, -limit, limit).astype(kind)


def setup_inputs(seed: int = 0, part: int = 0) -> dict:
    key_of = jax.random.split(jax.random.key(seed), 10)
    part_splits = jax.random.split(jax.random.fold_in(key_of[9], part), 10)
    tokens = centred(part_splits[0], (TOKENS, D), 1.0, 6.0, ((0, 32),))
    expert_ids_keys = jax.random.split(jax.random.fold_in(part_splits[1], 1), TOKENS // TOK_DEV)
    expert_ids_turns = jax.random.permutation(jax.random.fold_in(part_splits[1], 3), TOKENS // TOK_DEV)
    expert_ids = jax.vmap(lambda own, number: routed_block(jax.random.fold_in(part_splits[1], 2), own, number, TOK_DEV, EXPERTS, TOP, CAP, 2))(expert_ids_keys, expert_ids_turns).reshape((TOKENS, TOP))
    route_weight = jnp.clip(0.05 + 0.45 * jax.random.uniform(part_splits[2], (TOKENS, TOP), jnp.float32) ** block_levels(part_splits[2], (TOKENS, TOP), ((0, 32),), -0.2, 0.2), 0.05, 0.5)
    w_gate = centred(key_of[3], (EXPERTS, D, EH), D ** -0.5, 0.09375, ((0, 16), (2, 2)))
    w_up = centred(key_of[4], (EXPERTS, D, EH), D ** -0.5, 0.09375, ((0, 16), (2, 2)))
    w_down = centred(key_of[5], (EXPERTS, EH, D), EH ** -0.5, 0.1875, ((0, 16), (1, 2)))
    s_gate = centred(key_of[6], (D, SH), D ** -0.5, 0.09375, ((1, 4),))
    s_up = centred(key_of[7], (D, SH), D ** -0.5, 0.09375, ((1, 4),))
    s_down = centred(key_of[8], (SH, D), SH ** -0.5, 0.125, ((0, 4),))
    return dict(tokens=tokens, expert_ids=expert_ids, route_weight=route_weight, w_gate=w_gate, w_up=w_up, w_down=w_down, s_gate=s_gate, s_up=s_up, s_down=s_down)


def reference(tokens, expert_ids, route_weight, w_gate, w_up, w_down, s_gate, s_up, s_down):
    highest = lax.Precision.HIGHEST
    tokens_wide = tokens.astype(jnp.float32)
    shared_gate = jnp.dot(tokens_wide, s_gate.astype(jnp.float32), precision=highest)
    shared_upper = jnp.dot(tokens_wide, s_up.astype(jnp.float32), precision=highest)
    shared_hidden = (jax.nn.silu(shared_gate) * shared_upper).astype(jnp.bfloat16)
    shared_hidden = lax.optimization_barrier(shared_hidden).astype(jnp.float32)
    shared = jnp.dot(shared_hidden, s_down.astype(jnp.float32), precision=highest)
    rows_most = min(TOKENS, N_EXPERT * N_TENSOR * N_PAIR * CAP)
    slice_width = EH // N_TENSOR

    def expert_step(total, expert):
        matches = expert_ids == expert
        coefficient = jnp.sum(jnp.where(matches, route_weight, 0.0), axis=1)
        chosen = jnp.any(matches, axis=1)
        row_order = jnp.argsort(jnp.where(chosen, 0, 1).astype(jnp.int32), stable=True)[:rows_most].astype(jnp.int32)
        picked = tokens_wide[row_order]
        gate_part = jnp.dot(picked, w_gate[expert].astype(jnp.float32), precision=highest)
        upper_part = jnp.dot(picked, w_up[expert].astype(jnp.float32), precision=highest)
        hidden = (jax.nn.silu(gate_part) * upper_part).astype(jnp.bfloat16)
        hidden = lax.optimization_barrier(hidden).astype(jnp.float32)
        down_rows = w_down[expert].astype(jnp.float32).reshape(N_TENSOR, slice_width, D)
        pieces = jnp.einsum("rjh,jhd->jrd", hidden.reshape(rows_most, N_TENSOR, slice_width), down_rows, precision=highest)
        pieces = lax.optimization_barrier(pieces.astype(jnp.bfloat16)).astype(jnp.float32)
        result = lax.optimization_barrier(jnp.sum(pieces, axis=0).astype(jnp.bfloat16)).astype(jnp.float32)
        total = total.at[row_order].add(result * coefficient[row_order][:, None])
        return total, None

    routed, _ = lax.scan(expert_step, jnp.zeros((TOKENS, D), jnp.float32), jnp.arange(EXPERTS, dtype=jnp.int32))
    return (shared + routed).astype(jnp.bfloat16)
```

```python
import functools

import jax
import jax.numpy as jnp
from jax import lax
from jax.experimental import pallas as pl
from jax.experimental.pallas import tpu as pltpu
from jax.sharding import PartitionSpec as P

LANES = 128
VMEM_LIMIT = 48 * 1024 * 1024


def split_of(width):
    for parts in (4, 7, 2):
        if width % (parts * LANES) == 0:
            return parts
    return 1


def code_width(experts):
    return -(-2 * experts // LANES) * LANES


def pack_body(tokens_ref, ids_ref, weight_ref, out_ref):
    rows, model = tokens_ref.shape
    width = out_ref.shape[1] - model
    half = width // 2
    lane = lax.broadcasted_iota(jnp.int32, (rows, width), 1)
    place = jnp.where(lane < half, lane, lane - half)
    combine = jnp.zeros((rows, width), jnp.float32)
    for k in range(ids_ref.shape[1]):
        combine += jnp.where(place == ids_ref[:, k : k + 1], weight_ref[:, k : k + 1], 0.0)
    high = combine.astype(jnp.bfloat16).astype(jnp.float32)
    out_ref[:, :model] = tokens_ref[...]
    out_ref[:, model:] = jnp.where(lane < half, high, combine - high).astype(jnp.bfloat16)


def pack(tokens, expert_ids, route_weight, width):
    rows, model = tokens.shape
    return pl.pallas_call(
        pack_body,
        out_shape=jax.ShapeDtypeStruct((rows, model + width), jnp.bfloat16),
        name="pack",
    )(tokens, expert_ids, route_weight)


def ffn_body(steps, model, routed, adds, own_ref, *refs):
    refs = list(refs)
    xa_ref, xb_ref = refs.pop(0), refs.pop(0)
    if routed:
        ca_ref, cb_ref = refs.pop(0), refs.pop(0)
    wg_ref, wu_ref, wd_ref = refs.pop(0), refs.pop(0), refs.pop(0)
    if adds:
        sa_ref, sb_ref = refs.pop(0), refs.pop(0)
    oa_ref, ob_ref, gate, upper, hidden = refs
    rows = xa_ref.shape[0]
    step = pl.program_id(0)

    @pl.when(step < steps)
    def _():
        x = jnp.concatenate([xa_ref[...], xb_ref[...]], axis=0)
        g = jnp.dot(x, wg_ref[...], preferred_element_type=jnp.float32)
        u = jnp.dot(x, wu_ref[...], preferred_element_type=jnp.float32)

        @pl.when(step == 0)
        def _():
            gate[...] = g
            upper[...] = u

        @pl.when(step > 0)
        def _():
            gate[...] += g
            upper[...] += u

    @pl.when(step == steps - 1)
    def _():
        hidden[...] = (jax.nn.silu(gate[...]) * upper[...]).astype(jnp.bfloat16)

    @pl.when(step >= steps)
    def _():
        y = jnp.dot(hidden[...], wd_ref[...], preferred_element_type=jnp.float32)
        if routed:
            width = ca_ref.shape[1]
            lane = lax.broadcasted_iota(jnp.int32, (2 * rows, width), 1)
            mine = (lane == own_ref[0]) | (lane == own_ref[0] + width // 2)
            code = jnp.concatenate([ca_ref[...], cb_ref[...]], axis=0).astype(jnp.float32)
            y = y * jnp.sum(jnp.where(mine, code, 0.0), axis=1, keepdims=True)
        ya, yb = y[:rows], y[rows:]
        oa_ref[...] = ya.astype(oa_ref.dtype)
        ob_ref[...] = yb.astype(ob_ref.dtype)
        if adds:
            n = sa_ref.shape[0]
            oa_ref[:n, :] = (ya[:n] + sa_ref[...]).astype(oa_ref.dtype)
            ob_ref[:n, :] = (yb[:n] + sb_ref[...]).astype(ob_ref.dtype)


def ffn(xa, xb, own, w_gate, w_up, w_down, out_dtype, routed, extra=None, name="ffn"):
    rows = xa.shape[0]
    model, hid = w_gate.shape[-2:]
    steps = split_of(model)
    tile = model // steps
    lead = w_gate.ndim - 2
    first = lambda i, own: (0, jnp.minimum(i, steps - 1))
    second = lambda i, own: (0, jnp.maximum(i - steps, 0))
    w_first = lambda i, own: (0,) * lead + (jnp.minimum(i, steps - 1), 0)
    w_second = lambda i, own: (0,) * lead + (0, jnp.maximum(i - steps, 0))
    squeeze = (None,) * lead
    in_specs = [pl.BlockSpec((rows, tile), first)] * 2
    args = [xa, xb]
    if routed:
        width = xa.shape[1] - model
        in_specs += [pl.BlockSpec((rows, width), lambda i, own: (0, model // width))] * 2
        args += [xa, xb]
    in_specs += [pl.BlockSpec(squeeze + (tile, hid), w_first)] * 2
    in_specs += [pl.BlockSpec(squeeze + (hid, tile), w_second)]
    args += [w_gate, w_up, w_down]
    if extra is not None:
        in_specs += [pl.BlockSpec((extra[0].shape[0], tile), second)] * 2
        args += list(extra)
    out = jax.ShapeDtypeStruct((rows, model), out_dtype)
    return pl.pallas_call(
        functools.partial(ffn_body, steps, model, routed, extra is not None),
        out_shape=(out, out),
        grid_spec=pltpu.PrefetchScalarGridSpec(
            num_scalar_prefetch=1,
            grid=(2 * steps,),
            in_specs=in_specs,
            out_specs=[pl.BlockSpec((rows, tile), second)] * 2,
            scratch_shapes=[
                pltpu.VMEM((2 * rows, hid), jnp.float32),
                pltpu.VMEM((2 * rows, hid), jnp.float32),
                pltpu.VMEM((2 * rows, hid), jnp.bfloat16),
            ],
        ),
        compiler_params=pltpu.CompilerParams(vmem_limit_bytes=VMEM_LIMIT),
        cost_estimate=pl.CostEstimate(
            flops=12 * rows * model * hid,
            bytes_accessed=6 * model * hid + 8 * rows * model,
            transcendentals=2 * rows * hid,
        ),
        name=name,
    )(own, *args)


def sum_body(plan, n_in, *refs):
    ins, outs = refs[:n_in], refs[n_in:]
    for out_ref, terms in zip(outs, plan):
        total = None
        for index, start in terms:
            part = ins[index][start : start + out_ref.shape[0], :].astype(jnp.float32)
            total = part if total is None else total + part
        out_ref[...] = total.astype(out_ref.dtype)


def sums(arrays, plan, rows, dtypes, name):
    model = arrays[0].shape[1]
    parts = split_of(model)
    tile = model // parts
    return pl.pallas_call(
        functools.partial(sum_body, plan, len(arrays)),
        out_shape=tuple(jax.ShapeDtypeStruct((rows, model), d) for d in dtypes),
        grid=(parts,),
        in_specs=[pl.BlockSpec((a.shape[0], tile), lambda i: (0, i)) for a in arrays],
        out_specs=tuple(pl.BlockSpec((rows, tile), lambda i: (0, i)) for _ in dtypes),
        compiler_params=pltpu.CompilerParams(vmem_limit_bytes=VMEM_LIMIT),
        cost_estimate=pl.CostEstimate(
            flops=sum(a.size for a in arrays),
            bytes_accessed=4 * sum(a.size for a in arrays),
            transcendentals=0,
        ),
        name=name,
    )(*arrays)


def swap(size, by):
    if size & (size - 1) == 0:
        return [(i, i ^ by) for i in range(size)]
    return [(i, (i + by) % size) for i in range(size)]


def swap_back(size, by):
    return [(to, fro) for fro, to in swap(size, by)]


def per_device(tokens, expert_ids, route_weight, w_gate, w_up, w_down, s_gate, s_up, s_down):
    rows, model = tokens.shape
    n_expert = lax.axis_size("expert")
    n_tensor = lax.axis_size("tensor")
    n_pair = lax.axis_size("pair")
    assert n_pair == 2
    near = 2 if n_expert % 2 == 0 else 1
    far = n_expert // near

    def far_perm(by, back):
        table = swap_back(far, by) if back else swap(far, by)
        return [(a * near + c, b * near + c) for a, b in table for c in range(near)]

    def near_perm():
        return [(a * near + c, a * near + (c ^ 1)) for a in range(far) for c in range(near)]

    def go_far(t, by, back=False):
        return lax.ppermute(t, "expert", far_perm(by, back))

    def go_near(t):
        return lax.ppermute(t, "expert", near_perm())

    def go_tensor(t, by, back=False):
        return lax.ppermute(t, "tensor", (swap_back if back else swap)(n_tensor, by))

    def go_pair(t):
        return lax.ppermute(t, "pair", [(0, 1), (1, 0)])

    own = (lax.axis_index("expert") * n_pair + lax.axis_index("pair")).astype(jnp.int32)
    own = own.reshape(1)
    width = code_width(n_expert * n_pair)
    block = pack(tokens, expert_ids, route_weight, width)

    column = [block] + [go_far(block, k) for k in range(1, far)]
    blocks = {(0, 0): column}
    for j in range(1, n_tensor):
        blocks[j, 0] = [go_tensor(t, j) for t in column]
    if near == 2:
        blocks[0, 1] = [go_near(t) for t in column]
        for j in range(1, n_tensor):
            blocks[j, 1] = [
                go_near(blocks[j, 0][k]) if k % 2 == 0 else go_tensor(blocks[0, 1][k], j)
                for k in range(far)
            ]

    group = jnp.concatenate([blocks[j, 0][0] for j in range(n_tensor)], axis=0)
    shared = ffn(
        group, go_pair(group), own, s_gate, s_up, s_down, jnp.float32, False, name="shared"
    )

    mine, theirs = {}, {}
    for (j, i), group in blocks.items():
        group = jnp.concatenate(group, axis=0)
        extra = None
        if i == 0:
            extra = [s[j * rows : (j + 1) * rows] for s in shared]
        mine[j, i], other = ffn(
            group, go_pair(group), own, w_gate, w_up, w_down, jnp.bfloat16, True, extra,
            name="routed",
        )
        theirs[j, i] = go_pair(other)

    wide = [jnp.bfloat16] * far
    coming = {}
    if near == 2:
        for j in range(1, n_tensor):
            plan = [[(0, k * rows), (1, k * rows)] for k in range(far)]
            out = sums([mine[j, 1], theirs[j, 1]], plan, rows, wide, "sum_diagonal")
            coming[j] = [
                go_near(out[k]) if k % 2 == 0 else go_tensor(out[k], j, True) for k in range(far)
            ]
    returned = [[] for _ in range(far)]
    for j in range(1, n_tensor):
        arrays = [mine[j, 0], theirs[j, 0]]
        plan = [[(0, k * rows), (1, k * rows)] for k in range(far)]
        if near == 2:
            for k in range(0, far, 2):
                plan[k].append((len(arrays), 0))
                arrays.append(coming[j][k])
        out = sums(arrays, plan, rows, wide, "sum_tensor")
        for k in range(far):
            returned[k].append(go_tensor(out[k], j, True))
    if near == 2:
        arrays = [mine[0, 1], theirs[0, 1]]
        plan = [[(0, k * rows), (1, k * rows)] for k in range(far)]
        for j in range(1, n_tensor):
            for k in range(1, far, 2):
                plan[k].append((len(arrays), 0))
                arrays.append(coming[j][k])
        out = sums(arrays, plan, rows, wide, "sum_near")
        for k in range(far):
            returned[k].append(go_near(out[k]))
    arrays = [mine[0, 0], theirs[0, 0]]
    plan = [[(0, k * rows), (1, k * rows)] for k in range(far)]
    for k in range(far):
        for t in returned[k]:
            plan[k].append((len(arrays), 0))
            arrays.append(t)
    out = sums(arrays, plan, rows, [jnp.float32] + wide[1:], "sum_column")
    last = [out[0]] + [go_far(out[k], k, True) for k in range(1, far)]
    return sums(last, [[(n, 0) for n in range(far)]], rows, [jnp.bfloat16], "sum_far")[0]


def solution(mesh):
    in_specs = (
        P(("groups", "expert", "tensor", "pair"), None),
        P(("groups", "expert", "tensor", "pair"), None),
        P(("groups", "expert", "tensor", "pair"), None),
        P(("expert", "pair"), None, "tensor"),
        P(("expert", "pair"), None, "tensor"),
        P(("expert", "pair"), "tensor", None),
        P(None, ("tensor", "pair")),
        P(None, ("tensor", "pair")),
        P(("tensor", "pair"), None),
    )
    out_specs = P(("groups", "expert", "tensor", "pair"), None)
    return jax.shard_map(
        per_device, mesh=mesh, in_specs=in_specs, out_specs=out_specs, check_vma=False
    )
```

```python
import functools

import jax
import jax.numpy as jnp
from jax import lax
from jax.experimental import pallas as pl
from jax.experimental.pallas import tpu as pltpu
from jax.sharding import PartitionSpec as P

LANES = 128
VMEM_LIMIT = 20 * 1024 * 1024
IN_VMEM = pl.BlockSpec(memory_space=pltpu.VMEM)


def split_of(width):
    for parts in (4, 7, 2):
        if width % (parts * LANES) == 0:
            return parts
    return 1


def params():
    return pltpu.CompilerParams(vmem_limit_bytes=VMEM_LIMIT)


def pack_body(tokens_ref, ids_ref, weight_ref, out_ref):
    rows, model = tokens_ref.shape
    width = out_ref.shape[1] - model
    half = width // 2
    line = lax.broadcasted_iota(jnp.int32, (width, rows), 0)
    place = jnp.where(line < half, line, line - half)
    combine = jnp.zeros((width, rows), jnp.float32)
    for k in range(ids_ref.shape[0]):
        combine += jnp.where(place == ids_ref[k : k + 1, :], weight_ref[k : k + 1, :], 0.0)
    high = combine.astype(jnp.bfloat16).astype(jnp.float32)
    code = jnp.where(line < half, high, combine - high)
    out_ref[:, :model] = tokens_ref[...]
    out_ref[:, model:] = code.T.astype(jnp.bfloat16)


def pack(tokens, expert_ids, route_weight, width):
    rows, model = tokens.shape
    return pl.pallas_call(
        pack_body,
        out_shape=jax.ShapeDtypeStruct((rows, model + width), jnp.bfloat16),
        in_specs=[IN_VMEM] * 3,
        out_specs=IN_VMEM,
        name="pack",
    )(tokens, expert_ids.T, route_weight.T)


def ffn_body(n_parts, with_shared, share_of, index_ref, *refs):
    parts, refs = refs[: 2 * n_parts], refs[2 * n_parts :]
    wg_ref, wu_ref, wd_ref = refs[:3]
    if with_shared:
        sg_ref, su_ref, sd_ref = refs[3:6]
    oa_ref, ob_ref, x_ref = refs[-3:]
    rows, model = oa_ref.shape
    start = 0
    for part in parts:
        x_ref[start : start + part.shape[0], :] = part[...]
        start += part.shape[0]
    x = x_ref[:, :model]

    def hidden(g_ref, u_ref):
        g = jnp.dot(x, g_ref[...], preferred_element_type=jnp.float32)
        u = jnp.dot(x, u_ref[...], preferred_element_type=jnp.float32)
        return (jax.nn.silu(g) * u).astype(jnp.bfloat16)

    h = hidden(wg_ref, wu_ref)
    width = x_ref.shape[1] - model
    lane = lax.broadcasted_iota(jnp.int32, (2 * rows, width), 1)
    mine = (lane == index_ref[0]) | (lane == index_ref[0] + width // 2)
    code = x_ref[:, model:].astype(jnp.float32)
    scale = jnp.sum(jnp.where(mine, code, 0.0), axis=1, keepdims=True)
    if with_shared:
        s = hidden(sg_ref, su_ref)
        row = lax.broadcasted_iota(jnp.int32, (2 * rows, 1), 0)
        share = share_of(row, rows, index_ref[1])
    steps = split_of(model)
    tile = model // steps
    for i in range(steps):
        at = slice(i * tile, (i + 1) * tile)
        y = jnp.dot(h, wd_ref[:, at], preferred_element_type=jnp.float32) * scale
        if with_shared:
            more = jnp.dot(s, sd_ref[:, at], preferred_element_type=jnp.float32)
            y = y + jnp.where(share, more, 0.0)
        oa_ref[:, at] = y[:rows].astype(oa_ref.dtype)
        ob_ref[:, at] = y[rows:].astype(ob_ref.dtype)


def ffn(own_parts, other_parts, index, weights, share_of, name):
    rows = sum(p.shape[0] for p in own_parts)
    wide = own_parts[0].shape[1]
    hid, model = weights[2].shape
    out = jax.ShapeDtypeStruct((rows, model), jnp.bfloat16)
    parts = [*own_parts, *other_parts]
    return pl.pallas_call(
        functools.partial(ffn_body, len(own_parts), len(weights) > 3, share_of),
        out_shape=(out, out),
        in_specs=[pl.BlockSpec(memory_space=pltpu.SMEM)] + [IN_VMEM] * (len(parts) + len(weights)),
        out_specs=(IN_VMEM, IN_VMEM),
        scratch_shapes=[pltpu.VMEM((2 * rows, wide), jnp.bfloat16)],
        compiler_params=params(),
        cost_estimate=pl.CostEstimate(
            flops=4 * rows * model * hid * len(weights),
            bytes_accessed=8 * rows * model,
            transcendentals=2 * rows * hid,
        ),
        name=name,
    )(index, *parts, *weights)


def sum_body(starts, *refs):
    out_ref = refs[-1]
    total = None
    for ref, start in zip(refs, starts):
        part = ref[start : start + out_ref.shape[0], :].astype(jnp.float32)
        total = part if total is None else total + part
    out_ref[...] = total.astype(out_ref.dtype)


def sums(terms, rows, dtype, name):
    arrays = [a for a, _ in terms]
    model = arrays[0].shape[1]
    return pl.pallas_call(
        functools.partial(sum_body, [s for _, s in terms]),
        out_shape=jax.ShapeDtypeStruct((rows, model), dtype),
        in_specs=[IN_VMEM] * len(arrays),
        out_specs=IN_VMEM,
        compiler_params=params(),
        cost_estimate=pl.CostEstimate(
            flops=rows * model * len(arrays),
            bytes_accessed=2 * rows * model * len(arrays),
            transcendentals=0,
        ),
        name=name,
    )(*arrays)


def table(size, by):
    if size & (size - 1) == 0:
        return [i ^ by for i in range(size)]
    return [(i + by) % size for i in range(size)]


class Routes:
    axes = ("expert", "tensor", "pair")

    def __init__(self, n_expert, n_tensor, n_pair):
        self.sizes = (n_expert, n_tensor, n_pair)
        self.near = 2 if n_expert % 2 == 0 else 1
        self.far = n_expert // self.near
        self.colored = n_tensor == 2 and self.near == 2 and n_pair == 2

    def build(self, move):
        n_expert, n_tensor, n_pair = self.sizes
        out = []
        for e in range(n_expert):
            for t in range(n_tensor):
                for c in range(n_pair):
                    f, n = divmod(e, self.near)
                    f, n, t2, c2 = move(f, n, t, c)
                    out.append(((f * self.near + n) * n_tensor + t2) * n_pair + c2)
        return out

    def along_far(self, by):
        go = table(self.far, by)
        return self.build(lambda f, n, t, c: (go[f], n, t, c))

    def along_tensor(self, by):
        go = table(self.sizes[1], by)
        return self.build(lambda f, n, t, c: (f, n, go[t], c))

    def along_near(self):
        return self.build(lambda f, n, t, c: (f, n ^ 1, t, c))

    def other_core(self):
        return self.build(lambda f, n, t, c: (f, n, t, c ^ 1))

    def first(self):
        if self.colored:
            return [
                self.build(lambda f, n, t, c: (f, n, t ^ 1, c) if c == 0 else (f, n ^ 1, t, c))
            ]
        return [self.along_tensor(j) for j in range(1, self.sizes[1])]

    def second(self):
        if self.colored:
            return self.build(lambda f, n, t, c: (f, n ^ 1, t, c) if c == 0 else (f, n, t ^ 1, c))
        return self.along_near() if self.near == 2 else None

    def send(self, x, route):
        return lax.ppermute(x, self.axes, list(enumerate(route)))

    def send_back(self, x, route):
        return lax.ppermute(x, self.axes, [(to, fro) for fro, to in enumerate(route)])


def per_device(tokens, expert_ids, route_weight, w_gate, w_up, w_down, s_gate, s_up, s_down):
    rows, model = tokens.shape
    n_expert = lax.axis_size("expert")
    n_tensor = lax.axis_size("tensor")
    n_pair = lax.axis_size("pair")
    assert n_pair == 2
    routes = Routes(n_expert, n_tensor, n_pair)
    far = routes.far
    cross = routes.other_core()
    first, second = routes.first(), routes.second()

    core = lax.axis_index("pair")
    index = jnp.stack([lax.axis_index("expert") * n_pair + core, core]).astype(jnp.int32)
    pin = lambda w: pltpu.with_memory_space_constraint(w, pltpu.VMEM)
    routed_weights = [pin(w.reshape(w.shape[-2:])) for w in (w_gate, w_up, w_down)]
    shared_weights = [pin(w) for w in (s_gate, s_up, s_down)]
    width = -(-2 * n_expert * n_pair // LANES) * LANES
    block = pack(tokens, expert_ids, route_weight, width)

    def share_of(row, half, core):
        other = row >= half
        row = jnp.where(other, row - half, row)
        place = row // rows
        if not routes.colored:
            return place < n_tensor
        turn = jnp.where(other, 1 - core, core)
        return (place == 0) | (place == 1 + turn)

    order = list(range(far - 1, -1, -1))
    far_route = {k: routes.along_far(k) for k in range(1, far)}
    mine, theirs, head = {}, {}, {}
    for k in order:
        head[k] = routes.send(block, far_route[k]) if k else block
    for k in order:
        parts = [head[k]] + [routes.send(head[k], r) for r in first]
        if second is not None:
            parts.append(routes.send(jnp.concatenate(parts, axis=0), second))
        others = [routes.send(p, cross) for p in parts]
        weights = routed_weights + (shared_weights if k == 0 else [])
        mine[k], other = ffn(parts, others, index, weights, share_of, "ffn_%d" % k)
        theirs[k] = routes.send(other, cross)

    last = []
    for k in order:
        pair = [mine[k], theirs[k]]
        many = len(first) + 1
        terms = lambda start, more: [(a, start) for a in pair] + more
        came = []
        if second is not None:
            out = sums(terms(many * rows, []), many * rows, jnp.bfloat16, "sum_second")
            came = [routes.send_back(out, second)]
        home = []
        for j, r in enumerate(first):
            at = (j + 1) * rows
            out = sums(terms(at, [(a, at) for a in came]), rows, jnp.bfloat16, "sum_first")
            home.append(routes.send_back(out, r))
        dtype = jnp.bfloat16 if k else jnp.float32
        out = sums(terms(0, [(a, 0) for a in came + home]), rows, dtype, "sum_far")
        last.append(routes.send_back(out, far_route[k]) if k else out)
    return sums([(a, 0) for a in last], rows, jnp.bfloat16, "sum_last")


def solution(mesh):
    in_specs = (
        P(("groups", "expert", "tensor", "pair"), None),
        P(("groups", "expert", "tensor", "pair"), None),
        P(("groups", "expert", "tensor", "pair"), None),
        P(("expert", "pair"), None, "tensor"),
        P(("expert", "pair"), None, "tensor"),
        P(("expert", "pair"), "tensor", None),
        P(None, ("tensor", "pair")),
        P(None, ("tensor", "pair")),
        P(("tensor", "pair"), None),
    )
    out_specs = P(("groups", "expert", "tensor", "pair"), None)
    return jax.shard_map(
        per_device, mesh=mesh, in_specs=in_specs, out_specs=out_specs, check_vma=False
    )
```

```python
import functools

import jax
import jax.numpy as jnp
from jax import lax
from jax.experimental import pallas as pl
from jax.experimental.pallas import tpu as pltpu
from jax.sharding import PartitionSpec as P

LANES = 128
VMEM_LIMIT = 20 * 1024 * 1024
IN_VMEM = pl.BlockSpec(memory_space=pltpu.VMEM)


def split_of(width):
    for parts in (4, 7, 2):
        if width % (parts * LANES) == 0:
            return parts
    return 1


def params():
    return pltpu.CompilerParams(vmem_limit_bytes=VMEM_LIMIT)


def pack_body(tokens_ref, ids_ref, weight_ref, out_ref):
    rows, model = tokens_ref.shape
    width = out_ref.shape[1] - model
    half = width // 2
    line = lax.broadcasted_iota(jnp.int32, (width, rows), 0)
    place = jnp.where(line < half, line, line - half)
    combine = jnp.zeros((width, rows), jnp.float32)
    for k in range(ids_ref.shape[0]):
        combine += jnp.where(place == ids_ref[k : k + 1, :], weight_ref[k : k + 1, :], 0.0)
    high = combine.astype(jnp.bfloat16).astype(jnp.float32)
    code = jnp.where(line < half, high, combine - high)
    out_ref[:, :model] = tokens_ref[...]
    out_ref[:, model:] = code.T.astype(jnp.bfloat16)


def pack(tokens, expert_ids, route_weight, width):
    rows, model = tokens.shape
    return pl.pallas_call(
        pack_body,
        out_shape=jax.ShapeDtypeStruct((rows, model + width), jnp.bfloat16),
        in_specs=[IN_VMEM] * 3,
        out_specs=IN_VMEM,
        name="pack",
    )(tokens, expert_ids.T, route_weight.T)


def ffn_body(n_parts, n_weights, fresh, share_of, index_ref, *refs):
    parts, refs = refs[: 2 * n_parts], refs[2 * n_parts :]
    weights, refs = refs[:n_weights], refs[n_weights:]
    oa_ref, ob_ref = refs[:2]
    kept, x_ref = refs[2:5], refs[5]
    rows, model = oa_ref.shape
    steps = split_of(model)
    tile = model // steps
    copies = []
    if fresh:
        sems = refs[6]
        for i in range(steps):
            at = pl.ds(i * tile, tile)
            for n in (0, 1):
                copies.append(
                    pltpu.make_async_copy(weights[n].at[at], kept[n].at[at], sems.at[n, i])
                )
        size = weights[2].shape[0] // steps
        for i in range(steps):
            at = pl.ds(i * size, size)
            copies.append(pltpu.make_async_copy(weights[2].at[at], kept[2].at[at], sems.at[2, i]))
        for copy in copies:
            copy.start()
        weights = kept
    start = 0
    for part in parts:
        x_ref[start : start + part.shape[0], :] = part[...]
        start += part.shape[0]

    def hidden(g_ref, u_ref, waits=()):
        if not waits:
            x = x_ref[:, :model]
            g = jnp.dot(x, g_ref[...], preferred_element_type=jnp.float32)
            u = jnp.dot(x, u_ref[...], preferred_element_type=jnp.float32)
        else:
            g = u = jnp.zeros((2 * rows, g_ref.shape[1]), jnp.float32)
            for i in range(steps):
                at = slice(i * tile, (i + 1) * tile)
                for copy in waits[2 * i : 2 * i + 2]:
                    copy.wait()
                x = x_ref[:, at]
                g = g + jnp.dot(x, g_ref[at, :], preferred_element_type=jnp.float32)
                u = u + jnp.dot(x, u_ref[at, :], preferred_element_type=jnp.float32)
        return (jax.nn.silu(g) * u).astype(jnp.bfloat16)

    h = hidden(weights[0], weights[1], copies[: 2 * steps])
    width = x_ref.shape[1] - model
    lane = lax.broadcasted_iota(jnp.int32, (2 * rows, width), 1)
    mine = (lane == index_ref[0]) | (lane == index_ref[0] + width // 2)
    code = x_ref[:, model:].astype(jnp.float32)
    scale = jnp.sum(jnp.where(mine, code, 0.0), axis=1, keepdims=True)
    if n_weights > 3:
        s = hidden(weights[3], weights[4])
        row = lax.broadcasted_iota(jnp.int32, (2 * rows, 1), 0)
        share = share_of(row, rows, index_ref[1])
    for copy in copies[2 * steps :]:
        copy.wait()
    for i in range(steps):
        at = slice(i * tile, (i + 1) * tile)
        y = jnp.dot(h, weights[2][:, at], preferred_element_type=jnp.float32) * scale
        if n_weights > 3:
            more = jnp.dot(s, weights[5][:, at], preferred_element_type=jnp.float32)
            y = y + jnp.where(share, more, 0.0)
        oa_ref[:, at] = y[:rows].astype(oa_ref.dtype)
        ob_ref[:, at] = y[rows:].astype(ob_ref.dtype)


def ffn(own_parts, other_parts, index, weights, fresh, share_of, name):
    rows = sum(p.shape[0] for p in own_parts)
    wide = own_parts[0].shape[1]
    hid, model = weights[2].shape
    out = jax.ShapeDtypeStruct((rows, model), jnp.bfloat16)
    parts = [*own_parts, *other_parts]
    held = 0 if fresh else 3
    spaces = [pltpu.HBM if fresh else pltpu.VMEM] * 3 + [pltpu.VMEM] * (len(weights) - 3)
    weights = [pltpu.with_memory_space_constraint(w, s) for w, s in zip(weights, spaces)]
    scratch = [pltpu.VMEM((2 * rows, wide), jnp.bfloat16)]
    if fresh:
        scratch.append(pltpu.SemaphoreType.DMA((3, split_of(model))))
    return pl.pallas_call(
        functools.partial(ffn_body, len(own_parts), len(weights), fresh, share_of),
        out_shape=(out, out, *[pltpu.VMEM(w.shape, w.dtype) for w in weights[:3]]),
        in_specs=[pl.BlockSpec(memory_space=pltpu.SMEM)]
        + [IN_VMEM] * len(parts)
        + [pl.BlockSpec(memory_space=s) for s in spaces],
        out_specs=(IN_VMEM,) * 5,
        input_output_aliases={1 + len(parts) + i: 2 + i for i in range(held)},
        scratch_shapes=scratch,
        compiler_params=params(),
        cost_estimate=pl.CostEstimate(
            flops=4 * rows * model * hid * len(weights),
            bytes_accessed=8 * rows * model,
            transcendentals=2 * rows * hid,
        ),
        name=name,
    )(index, *parts, *weights)


def sum_body(starts, *refs):
    out_ref = refs[-1]
    total = None
    for ref, start in zip(refs, starts):
        part = ref[start : start + out_ref.shape[0], :].astype(jnp.float32)
        total = part if total is None else total + part
    out_ref[...] = total.astype(out_ref.dtype)


def sums(terms, rows, dtype, name):
    arrays = [a for a, _ in terms]
    model = arrays[0].shape[1]
    return pl.pallas_call(
        functools.partial(sum_body, [s for _, s in terms]),
        out_shape=jax.ShapeDtypeStruct((rows, model), dtype),
        in_specs=[IN_VMEM] * len(arrays),
        out_specs=IN_VMEM,
        compiler_params=params(),
        cost_estimate=pl.CostEstimate(
            flops=rows * model * len(arrays),
            bytes_accessed=2 * rows * model * len(arrays),
            transcendentals=0,
        ),
        name=name,
    )(*arrays)


def table(size, by):
    if size & (size - 1) == 0:
        return [i ^ by for i in range(size)]
    return [(i + by) % size for i in range(size)]


class Routes:
    axes = ("expert", "tensor", "pair")

    def __init__(self, n_expert, n_tensor, n_pair):
        self.sizes = (n_expert, n_tensor, n_pair)
        self.near = 2 if n_expert % 2 == 0 else 1
        self.far = n_expert // self.near
        self.colored = n_tensor == 2 and self.near == 2 and n_pair == 2

    def build(self, move):
        n_expert, n_tensor, n_pair = self.sizes
        out = []
        for e in range(n_expert):
            for t in range(n_tensor):
                for c in range(n_pair):
                    f, n = divmod(e, self.near)
                    f, n, t2, c2 = move(f, n, t, c)
                    out.append(((f * self.near + n) * n_tensor + t2) * n_pair + c2)
        return out

    def along_far(self, by):
        go = table(self.far, by)
        return self.build(lambda f, n, t, c: (go[f], n, t, c))

    def along_tensor(self, by):
        go = table(self.sizes[1], by)
        return self.build(lambda f, n, t, c: (f, n, go[t], c))

    def along_near(self):
        return self.build(lambda f, n, t, c: (f, n ^ 1, t, c))

    def other_core(self):
        return self.build(lambda f, n, t, c: (f, n, t, c ^ 1))

    def first(self):
        if self.colored:
            return [
                self.build(lambda f, n, t, c: (f, n, t ^ 1, c) if c == 0 else (f, n ^ 1, t, c))
            ]
        return [self.along_tensor(j) for j in range(1, self.sizes[1])]

    def second(self):
        if self.colored:
            return self.build(lambda f, n, t, c: (f, n ^ 1, t, c) if c == 0 else (f, n, t ^ 1, c))
        return self.along_near() if self.near == 2 else None

    def send(self, x, route):
        return lax.ppermute(x, self.axes, list(enumerate(route)))

    def send_back(self, x, route):
        return lax.ppermute(x, self.axes, [(to, fro) for fro, to in enumerate(route)])


def per_device(tokens, expert_ids, route_weight, w_gate, w_up, w_down, s_gate, s_up, s_down):
    rows, model = tokens.shape
    n_expert = lax.axis_size("expert")
    n_tensor = lax.axis_size("tensor")
    n_pair = lax.axis_size("pair")
    assert n_pair == 2
    routes = Routes(n_expert, n_tensor, n_pair)
    far = routes.far
    cross = routes.other_core()
    first, second = routes.first(), routes.second()

    core = lax.axis_index("pair")
    index = jnp.stack([lax.axis_index("expert") * n_pair + core, core]).astype(jnp.int32)
    weights = [w.reshape(w.shape[-2:]) for w in (w_gate, w_up, w_down)]
    shared = [s_gate, s_up, s_down]
    width = -(-2 * n_expert * n_pair // LANES) * LANES
    block = pack(tokens, expert_ids, route_weight, width)

    def share_of(row, half, core):
        other = row >= half
        row = jnp.where(other, row - half, row)
        place = row // rows
        if not routes.colored:
            return place < n_tensor
        turn = jnp.where(other, 1 - core, core)
        return (place == 0) | (place == 1 + turn)

    order = list(range(far - 1, -1, -1))
    far_route = {k: routes.along_far(k) for k in range(1, far)}
    many = len(first) + 1
    head, parts, others, pair, out = {}, {}, {}, {}, {}
    for k in order:
        head[k] = routes.send(block, far_route[k]) if k else block
    for k in order:
        parts[k] = [head[k]] + [routes.send(head[k], r) for r in first]
        if second is not None:
            parts[k].append(routes.send(jnp.concatenate(parts[k], axis=0), second))
        others[k] = [routes.send(p, cross) for p in parts[k]]

    came = {k: [] for k in order}
    home = {k: [] for k in order}
    last = []

    def compute(k):
        given = [*weights, *(shared if k == 0 else [])]
        fresh = k == order[0]
        mine, other, *kept = ffn(parts[k], others[k], index, given, fresh, share_of, "ffn_%d" % k)
        weights[:] = kept
        pair[k] = [mine, routes.send(other, cross)]

    def sum_second(k):
        if second is not None:
            at = many * rows
            out[k] = sums([(a, at) for a in pair[k]], at, jnp.bfloat16, "sum_second")

    def send_second(k):
        if second is not None:
            came[k] = [routes.send_back(out[k], second)]

    def sum_first(k):
        out[k] = [
            sums([(a, j * rows) for a in pair[k] + came[k]], rows, jnp.bfloat16, "sum_first")
            for j in range(1, many)
        ]

    def send_first(k):
        home[k] = [routes.send_back(o, r) for o, r in zip(out[k], first)]

    def sum_far(k):
        terms = [(a, 0) for a in pair[k] + came[k] + home[k]]
        out[k] = sums(terms, rows, jnp.bfloat16 if k else jnp.float32, "sum_far")

    def send_far(k):
        last.append(routes.send_back(out[k], far_route[k]) if k else out[k])

    def tie(a, b):
        return lax.optimization_barrier((a, b))

    for k in order[:-1]:
        compute(k)
        sum_second(k)
        send_second(k)
    lead = order[0]
    sum_first(lead)
    parts[0][0], out[lead][0] = tie(parts[0][0], out[lead][0])
    send_first(lead)
    compute(0)
    sum_second(0)
    sum_far(lead)
    send_far(lead)
    send_second(0)
    for k in order[1:-1]:
        sum_first(k)
        send_first(k)
        sum_far(k)
        send_far(k)
    sum_first(0)
    out[0][0], last[0] = tie(out[0][0], last[0])
    send_first(0)
    sum_far(0)
    send_far(0)
    return sums([(a, 0) for a in last], rows, jnp.bfloat16, "sum_last")


def solution(mesh):
    in_specs = (
        P(("groups", "expert", "tensor", "pair"), None),
        P(("groups", "expert", "tensor", "pair"), None),
        P(("groups", "expert", "tensor", "pair"), None),
        P(("expert", "pair"), None, "tensor"),
        P(("expert", "pair"), None, "tensor"),
        P(("expert", "pair"), "tensor", None),
        P(None, ("tensor", "pair")),
        P(None, ("tensor", "pair")),
        P(("tensor", "pair"), None),
    )
    out_specs = P(("groups", "expert", "tensor", "pair"), None)
    return jax.shard_map(
        per_device, mesh=mesh, in_specs=in_specs, out_specs=out_specs, check_vma=False
    )
```

```python
import functools

import jax
import jax.numpy as jnp
from jax import lax
from jax.experimental import pallas as pl
from jax.experimental.pallas import tpu as pltpu
from jax.sharding import PartitionSpec as P

LANES = 128
VMEM_LIMIT = 20 * 1024 * 1024
IN_VMEM = pl.BlockSpec(memory_space=pltpu.VMEM)


def split_of(width):
    for parts in (4, 7, 2):
        if width % (parts * LANES) == 0:
            return parts
    return 1


def params():
    return pltpu.CompilerParams(vmem_limit_bytes=VMEM_LIMIT)


def pack_body(tokens_ref, ids_ref, weight_ref, out_ref):
    rows, model = tokens_ref.shape
    width = out_ref.shape[1] - model
    half = width // 2
    line = lax.broadcasted_iota(jnp.int32, (width, rows), 0)
    place = jnp.where(line < half, line, line - half)
    combine = jnp.zeros((width, rows), jnp.float32)
    for k in range(ids_ref.shape[0]):
        combine += jnp.where(place == ids_ref[k : k + 1, :], weight_ref[k : k + 1, :], 0.0)
    high = combine.astype(jnp.bfloat16).astype(jnp.float32)
    code = jnp.where(line < half, high, combine - high)
    out_ref[:, :model] = tokens_ref[...]
    out_ref[:, model:] = code.T.astype(jnp.bfloat16)


def pack(tokens, expert_ids, route_weight, width):
    rows, model = tokens.shape
    return pl.pallas_call(
        pack_body,
        out_shape=jax.ShapeDtypeStruct((rows, model + width), jnp.bfloat16),
        in_specs=[IN_VMEM] * 3,
        out_specs=IN_VMEM,
        name="pack",
    )(tokens, expert_ids.T, route_weight.T)


def ffn_body(n_parts, n_weights, fresh, share_of, index_ref, *refs):
    parts, refs = refs[: 2 * n_parts], refs[2 * n_parts :]
    weights, refs = refs[:n_weights], refs[n_weights:]
    oa_ref, ob_ref = refs[:2]
    kept, x_ref = refs[2:5], refs[5]
    rows, model = oa_ref.shape
    steps = split_of(model)
    tile = model // steps
    copies = []
    if fresh:
        sems = refs[6]
        for i in range(steps):
            at = pl.ds(i * tile, tile)
            for n in (0, 1):
                copies.append(
                    pltpu.make_async_copy(weights[n].at[at], kept[n].at[at], sems.at[n, i])
                )
        size = weights[2].shape[0] // steps
        for i in range(steps):
            at = pl.ds(i * size, size)
            copies.append(pltpu.make_async_copy(weights[2].at[at], kept[2].at[at], sems.at[2, i]))
        for copy in copies:
            copy.start()
        weights = kept
    start = 0
    for part in parts:
        x_ref[start : start + part.shape[0], :] = part[...]
        start += part.shape[0]

    def hidden(g_ref, u_ref, waits=()):
        if not waits:
            x = x_ref[:, :model]
            g = jnp.dot(x, g_ref[...], preferred_element_type=jnp.float32)
            u = jnp.dot(x, u_ref[...], preferred_element_type=jnp.float32)
        else:
            g = u = jnp.zeros((2 * rows, g_ref.shape[1]), jnp.float32)
            for i in range(steps):
                at = slice(i * tile, (i + 1) * tile)
                for copy in waits[2 * i : 2 * i + 2]:
                    copy.wait()
                x = x_ref[:, at]
                g = g + jnp.dot(x, g_ref[at, :], preferred_element_type=jnp.float32)
                u = u + jnp.dot(x, u_ref[at, :], preferred_element_type=jnp.float32)
        return (jax.nn.silu(g) * u).astype(jnp.bfloat16)

    h = hidden(weights[0], weights[1], copies[: 2 * steps])
    width = x_ref.shape[1] - model
    lane = lax.broadcasted_iota(jnp.int32, (2 * rows, width), 1)
    mine = (lane == index_ref[0]) | (lane == index_ref[0] + width // 2)
    code = x_ref[:, model:].astype(jnp.float32)
    scale = jnp.sum(jnp.where(mine, code, 0.0), axis=1, keepdims=True)
    if n_weights > 3:
        s = hidden(weights[3], weights[4])
        row = lax.broadcasted_iota(jnp.int32, (2 * rows, 1), 0)
        share = share_of(row, rows, index_ref[1])
    for copy in copies[2 * steps :]:
        copy.wait()
    for i in range(steps):
        at = slice(i * tile, (i + 1) * tile)
        y = jnp.dot(h, weights[2][:, at], preferred_element_type=jnp.float32) * scale
        if n_weights > 3:
            more = jnp.dot(s, weights[5][:, at], preferred_element_type=jnp.float32)
            y = y + jnp.where(share, more, 0.0)
        oa_ref[:, at] = y[:rows].astype(oa_ref.dtype)
        ob_ref[:, at] = y[rows:].astype(ob_ref.dtype)


def ffn(own_parts, other_parts, index, weights, fresh, share_of, name):
    rows = sum(p.shape[0] for p in own_parts)
    wide = own_parts[0].shape[1]
    hid, model = weights[2].shape
    out = jax.ShapeDtypeStruct((rows, model), jnp.bfloat16)
    parts = [*own_parts, *other_parts]
    held = 0 if fresh else 3
    spaces = [pltpu.HBM if fresh else pltpu.VMEM] * 3 + [pltpu.VMEM] * (len(weights) - 3)
    weights = [pltpu.with_memory_space_constraint(w, s) for w, s in zip(weights, spaces)]
    scratch = [pltpu.VMEM((2 * rows, wide), jnp.bfloat16)]
    if fresh:
        scratch.append(pltpu.SemaphoreType.DMA((3, split_of(model))))
    return pl.pallas_call(
        functools.partial(ffn_body, len(own_parts), len(weights), fresh, share_of),
        out_shape=(out, out, *[pltpu.VMEM(w.shape, w.dtype) for w in weights[:3]]),
        in_specs=[pl.BlockSpec(memory_space=pltpu.SMEM)]
        + [IN_VMEM] * len(parts)
        + [pl.BlockSpec(memory_space=s) for s in spaces],
        out_specs=(IN_VMEM,) * 5,
        input_output_aliases={1 + len(parts) + i: 2 + i for i in range(held)},
        scratch_shapes=scratch,
        compiler_params=params(),
        cost_estimate=pl.CostEstimate(
            flops=4 * rows * model * hid * len(weights),
            bytes_accessed=8 * rows * model,
            transcendentals=2 * rows * hid,
        ),
        name=name,
    )(index, *parts, *weights)


def sum_body(starts, *refs):
    out_ref = refs[-1]
    total = None
    for ref, start in zip(refs, starts):
        part = ref[start : start + out_ref.shape[0], :].astype(jnp.float32)
        total = part if total is None else total + part
    out_ref[...] = total.astype(out_ref.dtype)


def sums(terms, rows, dtype, name):
    arrays = [a for a, _ in terms]
    model = arrays[0].shape[1]
    return pl.pallas_call(
        functools.partial(sum_body, [s for _, s in terms]),
        out_shape=jax.ShapeDtypeStruct((rows, model), dtype),
        in_specs=[IN_VMEM] * len(arrays),
        out_specs=IN_VMEM,
        compiler_params=params(),
        cost_estimate=pl.CostEstimate(
            flops=rows * model * len(arrays),
            bytes_accessed=2 * rows * model * len(arrays),
            transcendentals=0,
        ),
        name=name,
    )(*arrays)


def table(size, by):
    if size & (size - 1) == 0:
        return [i ^ by for i in range(size)]
    return [(i + by) % size for i in range(size)]


class Routes:
    axes = ("expert", "tensor", "pair")

    def __init__(self, n_expert, n_tensor, n_pair):
        self.sizes = (n_expert, n_tensor, n_pair)
        self.near = 2 if n_expert % 2 == 0 else 1
        self.far = n_expert // self.near
        self.colored = n_tensor == 2 and self.near == 2 and n_pair == 2

    def build(self, move):
        n_expert, n_tensor, n_pair = self.sizes
        out = []
        for e in range(n_expert):
            for t in range(n_tensor):
                for c in range(n_pair):
                    f, n = divmod(e, self.near)
                    f, n, t2, c2 = move(f, n, t, c)
                    out.append(((f * self.near + n) * n_tensor + t2) * n_pair + c2)
        return out

    def along_far(self, by):
        go = table(self.far, by)
        return self.build(lambda f, n, t, c: (go[f], n, t, c))

    def along_tensor(self, by):
        go = table(self.sizes[1], by)
        return self.build(lambda f, n, t, c: (f, n, go[t], c))

    def along_near(self):
        return self.build(lambda f, n, t, c: (f, n ^ 1, t, c))

    def other_core(self):
        return self.build(lambda f, n, t, c: (f, n, t, c ^ 1))

    def first(self):
        if self.colored:
            return [
                self.build(lambda f, n, t, c: (f, n, t ^ 1, c) if c == 0 else (f, n ^ 1, t, c))
            ]
        return [self.along_tensor(j) for j in range(1, self.sizes[1])]

    def second(self):
        if self.colored:
            return self.build(lambda f, n, t, c: (f, n ^ 1, t, c) if c == 0 else (f, n, t ^ 1, c))
        return self.along_near() if self.near == 2 else None

    def send(self, x, route):
        return lax.ppermute(x, self.axes, list(enumerate(route)))

    def send_back(self, x, route):
        return lax.ppermute(x, self.axes, [(to, fro) for fro, to in enumerate(route)])


def per_device(tokens, expert_ids, route_weight, w_gate, w_up, w_down, s_gate, s_up, s_down):
    rows, model = tokens.shape
    n_expert = lax.axis_size("expert")
    n_tensor = lax.axis_size("tensor")
    n_pair = lax.axis_size("pair")
    assert n_pair == 2
    routes = Routes(n_expert, n_tensor, n_pair)
    far = routes.far
    cross = routes.other_core()
    first, second = routes.first(), routes.second()

    core = lax.axis_index("pair")
    index = jnp.stack([lax.axis_index("expert") * n_pair + core, core]).astype(jnp.int32)
    weights = [w.reshape(w.shape[-2:]) for w in (w_gate, w_up, w_down)]
    shared = [s_gate, s_up, s_down]
    width = -(-2 * n_expert * n_pair // LANES) * LANES
    block = pack(tokens, expert_ids, route_weight, width)

    def share_of(row, half, core):
        other = row >= half
        row = jnp.where(other, row - half, row)
        place = row // rows
        if not routes.colored:
            return place < n_tensor
        turn = jnp.where(other, 1 - core, core)
        return (place == 0) | (place == 1 + turn)

    order = [*range(far - 1, 1, -1), *range(min(far, 2))]
    assert far > 1
    far_route = {k: routes.along_far(k) for k in range(1, far)}
    many = len(first) + 1
    head, parts, others, pair, out = {}, {}, {}, {}, {}
    for k in order:
        head[k] = routes.send(block, far_route[k]) if k else block
    for k in order:
        parts[k] = [head[k]] + [routes.send(head[k], r) for r in first]
        if second is not None:
            parts[k].append(routes.send(jnp.concatenate(parts[k], axis=0), second))
        parts[k] = [jnp.concatenate(parts[k], axis=0)]
        others[k] = [routes.send(parts[k][0], cross)]

    came = {k: [] for k in order}
    home = {k: [] for k in order}
    last = []

    def compute(k):
        given = [*weights, *(shared if k == 0 else [])]
        fresh = k == order[0]
        mine, other, *kept = ffn(parts[k], others[k], index, given, fresh, share_of, "ffn_%d" % k)
        weights[:] = kept
        pair[k] = [mine, routes.send(other, cross)]

    def sum_second(k):
        if second is not None:
            at = many * rows
            out[k] = sums([(a, at) for a in pair[k]], at, jnp.bfloat16, "sum_second")

    def send_second(k):
        if second is not None:
            came[k] = [routes.send_back(out[k], second)]

    def sum_first(k):
        out[k] = [
            sums([(a, j * rows) for a in pair[k] + came[k]], rows, jnp.bfloat16, "sum_first")
            for j in range(1, many)
        ]

    def send_first(k):
        home[k] = [routes.send_back(o, r) for o, r in zip(out[k], first)]

    def sum_far(k):
        terms = [(a, 0) for a in pair[k] + came[k] + home[k]]
        out[k] = sums(terms, rows, jnp.bfloat16 if k else jnp.float32, "sum_far")

    def send_far(k):
        last.append(routes.send_back(out[k], far_route[k]) if k else out[k])

    def tie(a, b):
        return lax.optimization_barrier((a, b))

    lead, end = order[0], order[-1]
    for k in order[:-1]:
        compute(k)
        sum_second(k)
        send_second(k)
    sum_first(lead)
    parts[end][0], out[lead][0] = tie(parts[end][0], out[lead][0])
    send_first(lead)
    compute(end)
    sum_second(end)
    sum_far(lead)
    send_far(lead)
    send_second(end)
    for k in order[1:-1]:
        sum_first(k)
        send_first(k)
        sum_far(k)
        send_far(k)
    sum_first(end)
    out[end][0], last[0] = tie(out[end][0], last[0])
    send_first(end)
    sum_far(end)
    send_far(end)
    return sums([(a, 0) for a in last], rows, jnp.bfloat16, "sum_last")


def solution(mesh):
    in_specs = (
        P(("groups", "expert", "tensor", "pair"), None),
        P(("groups", "expert", "tensor", "pair"), None),
        P(("groups", "expert", "tensor", "pair"), None),
        P(("expert", "pair"), None, "tensor"),
        P(("expert", "pair"), None, "tensor"),
        P(("expert", "pair"), "tensor", None),
        P(None, ("tensor", "pair")),
        P(None, ("tensor", "pair")),
        P(("tensor", "pair"), None),
    )
    out_specs = P(("groups", "expert", "tensor", "pair"), None)
    return jax.shard_map(
        per_device, mesh=mesh, in_specs=in_specs, out_specs=out_specs, check_vma=False
    )
```
